512 devices in a mesh: layer: 4 (over x), seq: 16 (over y, core), tile: 8 (over z).
Axes of the slice: x: 4, y: 8, z: 8, core: 2. Of those that a mesh axis runs over, the one named last changes fastest.
Arguments:
- activations: bfloat16 [16, 3072, 4096], P('layer', 'seq', 'tile'), parts along dimension 0, may hold values from -6 to 6
- out_grads: bfloat16 [16, 3072, 14336], P('layer', 'seq', 'tile'), parts along dimension 0, may hold values from -6 to 6
- proj_in: bfloat16 [16384, 128], P(('layer', 'tile')), parts along dimension 0, may hold values from -0.09375 to 0.09375
- proj_out: bfloat16 [57344, 256], P(('layer', 'tile')), parts along dimension 0, may hold values from -0.046875 to 0.046875
- seq_lengths: int32 [4], replicated, may hold values from 1 to 3072, 7680 in all
- tile_map: int32 [128, 2], replicated, may hold values from 0 to 127, as said below
- prior_cov: float32 [512, 256, 256], P(('layer', 'seq', 'tile')), parts along dimension 0, may hold values from -6 to 6
Outputs:
- covariance: float32 [512, 256, 256], P(('layer', 'seq', 'tile')), parts along dimension 0
The draws below stay inside these ranges and needn't reach their ends.
There are 4 independent parts, one for each index of `layer`. The reference program is written for one: setup_inputs(seed, part) draws one part's arguments, and reference() takes and returns one part's arrays. A program takes and returns all parts, laid end to end along the dimension named above; an argument that names none is the same for every part. Nothing has to cross between parts.
Inputs may be any that keep to these rules, and one draw needn't show every extreme that they name: `tile_map`: each row holds two feature block numbers, the first not above the second; rows may repeat.
All inputs are finite; a program needn't handle non-finite values.
Results may differ from the reference program's by a relative error of at most 0.0003.
Values sent between devices are 32-bit elements; how exact they have to be, the bound alone decides.
No kernel may reach another device: no remote copies, remote signals or barrier semaphores. Data moves between devices by JAX's collectives and lax.ppermute only.
A program may use at most 192 MiB of HBM per device.

```python
import math
import jax
import jax.numpy as jnp
import numpy as np
from jax import lax

D = 4096
FF = 14336
K_IN = 128
K_OUT = 256
TB = 256
SEQS = 4
LEN_DEV = 192
LEN = 3072
NBLOCKS = 128
TILES = 128
N_SEQ = 16


def draw_tile_map(key, part):
    first_key, second_key = jax.random.split(jax.random.fold_in(key, 11))
    upper_draw = jax.random.randint(first_key, (TILES,), 0, NBLOCKS)
    lower_draw = jax.random.randint(second_key, (TILES,), 0, NBLOCKS)
    tile_rows = jnp.stack([jnp.minimum(upper_draw, lower_draw), jnp.maximum(upper_draw, lower_draw)], axis=1)
    tile_rows = tile_rows.at[0].set(jnp.array([0, NBLOCKS - 1], dtype=jnp.int32))
    return tile_rows.astype(jnp.int32)


def block_scale(own_key, extent, shards, low, largest):
    factor_of, own = 1.0, jax.random.fold_in(own_key, 6)
    for dim, shards_of in shards:
        heights = jnp.exp(jax.random.uniform(jax.random.fold_in(own, dim), (shards_of,), jnp.float32, low / len(shards), largest / len(shards)))
        factor_of = factor_of * jnp.repeat(heights, extent[dim] // shards_of).reshape([-1 if axis == dim else 1 for axis in range(len(extent))])
    return factor_of


def profile(count, total, most, lean):
    portions = [(1 << 20) // math.isqrt(rank ** lean) + 1 for rank in range(2, count + 1)]
    rest, holding = total - most - (count - 1), [1] * (count - 1)
    while rest > 0:
        movable = [i for i in range(count - 1) if holding[i] < most]
        mass, remaining = sum([portions[i] for i in movable]), rest
        for i in movable:
            addition = min(most - holding[i], max(1, remaining * portions[i] // mass), rest)
            holding[i] = holding[i] + addition
            rest = rest - addition
    return np.array([most] + holding)


def ragged(key, count, total, bound, slope):
    if count == 2:
        one = jax.random.randint(key, (), max(1, total - bound), min(bound, total - 1) + 1)
        return jnp.stack([one, total - one])
    sizes = jnp.asarray(profile(count, total, bound, slope), jnp.int32)
    twos = (count - 1) // 2
    source_of, sink = sizes[1:1 + 2 * twos:2], sizes[2:2 + 2 * twos:2]
    margin = jnp.minimum(source_of - 1, bound - sink)
    passed = jax.random.randint(jax.random.fold_in(key, 1), (twos,), 0, 1 << 20) % (margin + 1)
    sizes = sizes.at[1:1 + 2 * twos:2].set(source_of - passed).at[2:2 + 2 * twos:2].set(sink + passed)
    return sizes[jax.random.permutation(jax.random.fold_in(key, 2), count)]


def scatter_about(stream_key, extent, width, most, shards=(), kind=jnp.bfloat16):
    result = width * jax.random.normal(stream_key, extent, jnp.float32)
    if shards:
        result = result * block_scale(stream_key, extent, shards, -0.22, 0.18)
    return jnp.clip(result, -most, most).astype(kind)


def setup_inputs(seed: int = 0, part: int = 0) -> dict:
    splits = jax.random.split(jax.random.key(seed), 8)
    part_splits = jax.random.split(jax.random.fold_in(splits[7], part), 8)
    return {
        "activations": scatter_about(part_splits[0], (SEQS, LEN, D), 1.0, 6.0, ((1, 16), (2, 8))),
        "out_grads": scatter_about(part_splits[1], (SEQS, LEN, FF), 1.0, 6.0, ((1, 16), (2, 8))),
        "proj_in": scatter_about(part_splits[2], (D, K_IN), D ** -0.5, 0.09375, ((0, 8),)),
        "proj_out": scatter_about(part_splits[3], (FF, K_OUT), FF ** -0.5, 0.046875, ((0, 8),)),
        "seq_lengths": ragged(splits[4], SEQS, SEQS * LEN_DEV * N_SEQ * 5 // 8, LEN_DEV * N_SEQ, 1).astype(jnp.int32),
        "tile_map": draw_tile_map(jax.random.fold_in(splits[7], 71), part),
        "prior_cov": scatter_about(part_splits[6], (TILES, TB, TB), 1.0, 6.0, ((0, 128),), jnp.float32),
    }


def reference(activations, out_grads, proj_in, proj_out, seq_lengths, tile_map, prior_cov):
    positions = jnp.arange(LEN, dtype=jnp.int32)

    def one_sequence(inputs):
        seq_acts, seq_grads, length = inputs
        left_side = jnp.dot(seq_acts, proj_in, preferred_element_type=jnp.float32)
        right_side = jnp.dot(seq_grads, proj_out, preferred_element_type=jnp.float32)
        token_mask = (positions < length).astype(jnp.float32)
        right_side = right_side * token_mask[:, None]
        grad_matrix = jnp.dot(right_side.T, left_side, precision=lax.Precision.HIGHEST)
        grad_matrix = grad_matrix * lax.rsqrt(length.astype(jnp.float32))
        return grad_matrix.reshape(-1)
    example_grads = lax.map(one_sequence, (activations, out_grads, seq_lengths))
    blocks = example_grads.reshape(SEQS, NBLOCKS, TB)
    left_blocks = blocks[:, tile_map[:, 0], :]
    right_blocks = blocks[:, tile_map[:, 1], :]
    return prior_cov + jnp.einsum('ske,skf->kef', left_blocks, right_blocks, precision=lax.Precision.HIGHEST)
```

```python
import functools

import jax
import jax.numpy as jnp
from jax import lax
from jax.experimental import pallas as pl
from jax.experimental.pallas import tpu as pltpu
from jax.sharding import Mesh
from jax.sharding import PartitionSpec as P

HIGHEST = lax.Precision.HIGHEST
VMEM_LIMIT = 32 * 1024 * 1024


def project_kernel(act_ref, grad_ref, in_ref, out_ref, o_ref):
    width_in = in_ref.shape[1]
    pieces, _, rows, width = o_ref.shape
    left = jnp.dot(act_ref[0], in_ref[...], preferred_element_type=jnp.float32)
    right = jnp.dot(grad_ref[0], out_ref[...], preferred_element_type=jnp.float32)
    o_ref[:, 0, :, :width_in] = left.reshape(pieces, rows, width_in)
    o_ref[:, 0, :, width_in:] = right.reshape(pieces, rows, width - width_in)


def project(activations, out_grads, proj_in, proj_out, pieces):
    seqs, tok, dim = activations.shape
    hidden = out_grads.shape[2]
    width_in, width_out = proj_in.shape[1], proj_out.shape[1]
    rows, width = tok // pieces, width_in + width_out
    return pl.pallas_call(
        project_kernel,
        grid=(seqs,),
        out_shape=jax.ShapeDtypeStruct((pieces, seqs, rows, width), jnp.float32),
        in_specs=[
            pl.BlockSpec((1, tok, dim), lambda s: (s, 0, 0)),
            pl.BlockSpec((1, tok, hidden), lambda s: (s, 0, 0)),
            pl.BlockSpec((dim, width_in), lambda s: (0, 0)),
            pl.BlockSpec((hidden, width_out), lambda s: (0, 0)),
        ],
        out_specs=pl.BlockSpec((pieces, 1, rows, width), lambda s: (0, s, 0, 0)),
        compiler_params=pltpu.CompilerParams(vmem_limit_bytes=VMEM_LIMIT),
        cost_estimate=pl.CostEstimate(
            flops=2 * seqs * tok * (dim * width_in + hidden * width_out),
            bytes_accessed=2 * seqs * tok * (dim + hidden) + 4 * seqs * tok * width,
            transcendentals=0,
        ),
    )(activations, out_grads, proj_in, proj_out)


def expand_kernel(map_ref, core_ref, own_ref, other_ref, o_ref, grads_ref):
    seqs = own_ref.shape[0]
    width_in = o_ref.shape[1]
    width_out = own_ref.shape[2] - width_in
    for s in range(seqs):
        tokens = jnp.concatenate([own_ref[s], other_ref[s]], axis=0)
        left, right = tokens[:, :width_in], tokens[:, width_in:]
        grads_ref[pl.ds(s, width_out, stride=seqs), :] = lax.dot_general(
            right, left, (((0,), (0,)), ((), ())), precision=HIGHEST, preferred_element_type=jnp.float32
        )
    core = core_ref[0]
    owners = o_ref.shape[0] // 16
    for n in range(owners):
        k = (2 * (n // 8) + core) * 8 + n % 8
        for side in range(2):
            block = map_ref[side, k]
            o_ref[16 * n + 8 * side:16 * n + 8 * side + 8, :] = grads_ref[
                pl.ds(pl.multiple_of(block * 8, 8), 8), :
            ]


def expand(tile_map, core, own, other, owners, width_in):
    seqs, rows, width = own.shape
    width_out = width - width_in
    return pl.pallas_call(
        expand_kernel,
        out_shape=jax.ShapeDtypeStruct((owners * 16, width_in), jnp.float32),
        in_specs=[
            pl.BlockSpec(memory_space=pltpu.SMEM),
            pl.BlockSpec(memory_space=pltpu.SMEM),
            pl.BlockSpec(memory_space=pltpu.VMEM),
            pl.BlockSpec(memory_space=pltpu.VMEM),
        ],
        out_specs=pl.BlockSpec(memory_space=pltpu.VMEM),
        scratch_shapes=[pltpu.VMEM((seqs * width_out, width_in), jnp.float32)],
        compiler_params=pltpu.CompilerParams(vmem_limit_bytes=VMEM_LIMIT),
        cost_estimate=pl.CostEstimate(
            flops=4 * seqs * rows * width_in * width_out,
            bytes_accessed=4 * (2 * seqs * rows * width + owners * 16 * width_in),
            transcendentals=0,
        ),
    )(tile_map.T, core, own, other)


def covariance_kernel(terms_ref, prior_ref, o_ref):
    blocks = jnp.sum(terms_ref[...], axis=0)
    left = jnp.concatenate([blocks[0:4], blocks[4:8]], axis=1)
    right = jnp.concatenate([blocks[8:12], blocks[12:16]], axis=1)
    product = lax.dot_general(
        left, right, (((0,), (0,)), ((), ())), precision=HIGHEST, preferred_element_type=jnp.float32
    )
    o_ref[0] = prior_ref[0] + product


def covariance(terms, prior_cov):
    return pl.pallas_call(
        covariance_kernel,
        out_shape=jax.ShapeDtypeStruct(prior_cov.shape, jnp.float32),
        in_specs=[pl.BlockSpec(memory_space=pltpu.VMEM)] * 2,
        out_specs=pl.BlockSpec(memory_space=pltpu.VMEM),
        compiler_params=pltpu.CompilerParams(vmem_limit_bytes=VMEM_LIMIT),
    )(terms, prior_cov)


def body(activations, out_grads, proj_in, proj_out, seq_lengths, tile_map, prior_cov):
    seqs, tok, _ = activations.shape
    width_in, width_out = proj_in.shape[1], proj_out.shape[1]
    pieces = lax.axis_size("tile")
    rows = tok // pieces
    width = width_in + width_out
    owners = lax.axis_size("y") * pieces
    partial = project(activations, out_grads, proj_in, proj_out, pieces)
    partial = partial.reshape(pieces, seqs * rows, width)
    arrived = lax.all_to_all(partial, "tile", 0, 0, tiled=True)
    summed = jnp.sum(arrived.reshape(pieces, seqs, rows, width), axis=0)
    core = lax.axis_index("core")
    positions = (
        (lax.axis_index("y") * 2 + core) * tok
        + lax.axis_index("tile") * rows
        + jnp.arange(rows, dtype=jnp.int32)
    )
    weight = jnp.where(
        positions[None, :] < seq_lengths[:, None],
        lax.rsqrt(seq_lengths.astype(jnp.float32))[:, None],
        0.0,
    )
    grad_side = lax.broadcasted_iota(jnp.int32, (1, 1, width), 2) >= width_in
    own = summed * jnp.where(grad_side, weight[:, :, None], 1.0)
    other = lax.ppermute(own, "core", [(0, 1), (1, 0)])
    terms = expand(tile_map, core.reshape(1).astype(jnp.int32), own, other, owners, width_in)
    terms = lax.all_to_all(terms, ("y", "tile"), 0, 0, tiled=True)
    return covariance(terms.reshape(owners, 16, width_in), prior_cov)


def solution(mesh):
    layers, seq, tile = (mesh.shape[name] for name in ("layer", "seq", "tile"))
    fine = Mesh(mesh.devices.reshape(layers, seq // 2, 2, tile), ("layer", "y", "core", "tile"))
    split = ("y", "core")
    return jax.shard_map(
        body,
        mesh=fine,
        in_specs=(
            P("layer", split, "tile"),
            P("layer", split, "tile"),
            P(("layer", "tile"), None),
            P(("layer", "tile"), None),
            P(),
            P(),
            P(("layer", "y", "core", "tile"), None, None),
        ),
        out_specs=P(("layer", "y", "core", "tile"), None, None),
        check_vma=False,
    )
```

```python
import jax
import jax.numpy as jnp
from jax import lax
from jax.experimental import pallas as pl
from jax.experimental.pallas import tpu as pltpu
from jax.sharding import Mesh
from jax.sharding import PartitionSpec as P

HIGHEST = lax.Precision.HIGHEST
VMEM_LIMIT = 4 * 1024 * 1024
PROJECT_VMEM = 8 * 1024 * 1024


def project_kernel(x_ref, w_ref, o_ref):
    product = jnp.dot(x_ref[0], w_ref[...], preferred_element_type=jnp.float32)
    o_ref[...] = product


def project(x, w):
    seqs, tok, dim = x.shape
    width = w.shape[1]
    return pl.pallas_call(
        project_kernel,
        grid=(seqs,),
        out_shape=jax.ShapeDtypeStruct((seqs * tok, width), jnp.float32),
        in_specs=[
            pl.BlockSpec((1, tok, dim), lambda s: (s, 0, 0)),
            pl.BlockSpec((dim, width), lambda s: (0, 0)),
        ],
        out_specs=pl.BlockSpec((tok, width), lambda s: (s, 0)),
        compiler_params=pltpu.CompilerParams(vmem_limit_bytes=PROJECT_VMEM),
        cost_estimate=pl.CostEstimate(
            flops=2 * seqs * tok * dim * width,
            bytes_accessed=2 * seqs * tok * dim + 4 * seqs * tok * width,
            transcendentals=0,
        ),
    )(x, w)


def combine_kernel(terms_ref, weight_ref, right_ref, o_ref, held_ref):
    own = jnp.sum(terms_ref[...], axis=0) * weight_ref[...]
    for piece in range(o_ref.shape[0]):
        o_ref[piece] = own


def combine(terms, weight, right):
    return pl.pallas_call(
        combine_kernel,
        out_shape=(
            jax.ShapeDtypeStruct(terms.shape, jnp.float32),
            jax.ShapeDtypeStruct(right.shape, jnp.float32),
        ),
        in_specs=[pl.BlockSpec(memory_space=pltpu.VMEM)] * 3,
        out_specs=(pl.BlockSpec(memory_space=pltpu.VMEM),) * 2,
        input_output_aliases={2: 1},
        compiler_params=pltpu.CompilerParams(vmem_limit_bytes=VMEM_LIMIT),
    )(terms, weight, right)


def outer_kernel(left_ref, right_ref, o_ref):
    seqs, _, width_out = right_ref.shape
    for s in range(seqs):
        o_ref[pl.ds(s, width_out, stride=seqs), :] = lax.dot_general(
            right_ref[s], left_ref[s], (((0,), (0,)), ((), ())), precision=HIGHEST, preferred_element_type=jnp.float32
        )


def outer(left, right):
    seqs, _, width_in = left.shape
    width_out = right.shape[2]
    return pl.pallas_call(
        outer_kernel,
        out_shape=jax.ShapeDtypeStruct((seqs * width_out, width_in), jnp.float32),
        in_specs=[pl.BlockSpec(memory_space=pltpu.VMEM)] * 2,
        out_specs=pl.BlockSpec(memory_space=pltpu.VMEM),
        compiler_params=pltpu.CompilerParams(vmem_limit_bytes=VMEM_LIMIT),
    )(left, right)


def expand_kernel(map_ref, core_ref, own_ref, other_ref, o_ref):
    core = core_ref[0]
    owners = o_ref.shape[0] // 16
    for n in range(owners):
        k = (2 * (n // 8) + core) * 8 + n % 8
        for side in range(2):
            at = pl.ds(pl.multiple_of(map_ref[side, k] * 8, 8), 8)
            o_ref[16 * n + 8 * side:16 * n + 8 * side + 8, :] = own_ref[at, :] + other_ref[at, :]


def expand(tile_map, core, own, other, owners):
    return pl.pallas_call(
        expand_kernel,
        out_shape=jax.ShapeDtypeStruct((owners * 16, own.shape[1]), jnp.float32),
        in_specs=[
            pl.BlockSpec(memory_space=pltpu.SMEM),
            pl.BlockSpec(memory_space=pltpu.SMEM),
            pl.BlockSpec(memory_space=pltpu.VMEM),
            pl.BlockSpec(memory_space=pltpu.VMEM),
        ],
        out_specs=pl.BlockSpec(memory_space=pltpu.VMEM),
        compiler_params=pltpu.CompilerParams(vmem_limit_bytes=VMEM_LIMIT),
    )(tile_map.T, core, own, other)


def covariance_kernel(terms_ref, prior_ref, o_ref):
    blocks = jnp.sum(terms_ref[...], axis=0)
    left = jnp.concatenate([blocks[0:4], blocks[4:8]], axis=1)
    right = jnp.concatenate([blocks[8:12], blocks[12:16]], axis=1)
    product = lax.dot_general(
        left, right, (((0,), (0,)), ((), ())), precision=HIGHEST, preferred_element_type=jnp.float32
    )
    o_ref[0] = prior_ref[0] + product


def covariance(terms, prior_cov):
    return pl.pallas_call(
        covariance_kernel,
        out_shape=jax.ShapeDtypeStruct(prior_cov.shape, jnp.float32),
        in_specs=[pl.BlockSpec(memory_space=pltpu.VMEM)] * 2,
        out_specs=pl.BlockSpec(memory_space=pltpu.VMEM),
        compiler_params=pltpu.CompilerParams(vmem_limit_bytes=VMEM_LIMIT),
    )(terms, prior_cov)


def body(activations, out_grads, proj_in, proj_out, seq_lengths, tile_map, prior_cov):
    seqs, tok, _ = activations.shape
    width_in = proj_in.shape[1]
    pieces = lax.axis_size("tile")
    rows = seqs * tok // pieces
    owners = lax.axis_size("y") * pieces
    left = jnp.dot(activations.reshape(seqs * tok, -1), proj_in, preferred_element_type=jnp.float32)
    arrived = lax.all_to_all(left.reshape(pieces, rows, width_in), "tile", 0, 0, tiled=True)
    right = project(out_grads, proj_out)
    core = lax.axis_index("core")
    token = lax.axis_index("tile") * rows + jnp.arange(rows, dtype=jnp.int32)
    position = (lax.axis_index("y") * 2 + core) * tok + token % tok
    length = jnp.sum(jnp.where(token[:, None] // tok == jnp.arange(seqs)[None, :], seq_lengths[None, :], 0), axis=1)
    weight = jnp.where(position < length, lax.rsqrt(length.astype(jnp.float32)), 0.0)
    weight = jnp.broadcast_to(weight[:, None], (rows, width_in))
    arrived, right, weight = lax.optimization_barrier((arrived, right, weight))
    copies, right = combine(arrived, weight, right)
    left = lax.all_to_all(copies, "tile", 0, 0, tiled=True).reshape(seqs, tok, width_in)
    right = right.reshape(seqs, tok, -1)
    grads = outer(left, right)
    other = lax.ppermute(grads, "core", [(0, 1), (1, 0)])
    terms = expand(tile_map, core.reshape(1).astype(jnp.int32), grads, other, owners)
    terms = lax.all_to_all(terms.reshape(owners, 16, width_in), ("y", "tile"), 0, 0, tiled=True)
    return covariance(terms, prior_cov)


def solution(mesh):
    layers, seq, tile = (mesh.shape[name] for name in ("layer", "seq", "tile"))
    fine = Mesh(mesh.devices.reshape(layers, seq // 2, 2, tile), ("layer", "y", "core", "tile"))
    split = ("y", "core")
    return jax.shard_map(
        body,
        mesh=fine,
        in_specs=(
            P("layer", split, "tile"),
            P("layer", split, "tile"),
            P(("layer", "tile"), None),
            P(("layer", "tile"), None),
            P(),
            P(),
            P(("layer", "y", "core", "tile"), None, None),
        ),
        out_specs=P(("layer", "y", "core", "tile"), None, None),
        check_vma=False,
    )
```

```python
import functools

import jax
import jax.numpy as jnp
from jax import lax
from jax.experimental import pallas as pl
from jax.experimental.pallas import tpu as pltpu
from jax.sharding import Mesh
from jax.sharding import PartitionSpec as P

VMEM_LIMIT = 4 * 1024 * 1024
PROJECT_VMEM = 8 * 1024 * 1024


def project_kernel(x_ref, w_ref, o_ref):
    product = jnp.dot(x_ref[0], w_ref[...], preferred_element_type=jnp.float32)
    o_ref[...] = product


def project(x, w):
    seqs, tok, dim = x.shape
    width = w.shape[1]
    return pl.pallas_call(
        project_kernel,
        grid=(seqs,),
        out_shape=jax.ShapeDtypeStruct((seqs * tok, width), jnp.float32),
        in_specs=[
            pl.BlockSpec((1, tok, dim), lambda s: (s, 0, 0)),
            pl.BlockSpec((dim, width), lambda s: (0, 0)),
        ],
        out_specs=pl.BlockSpec((tok, width), lambda s: (s, 0)),
        compiler_params=pltpu.CompilerParams(vmem_limit_bytes=PROJECT_VMEM),
        cost_estimate=pl.CostEstimate(
            flops=2 * seqs * tok * dim * width,
            bytes_accessed=2 * seqs * tok * dim + 4 * seqs * tok * width,
            transcendentals=0,
        ),
    )(x, w)


def combine_kernel(terms_ref, weight_ref, right_ref, o_ref, held_ref):
    own = jnp.sum(terms_ref[...], axis=0) * weight_ref[...]
    for piece in range(o_ref.shape[0]):
        o_ref[piece] = own


def combine(terms, weight, right):
    return pl.pallas_call(
        combine_kernel,
        out_shape=(
            jax.ShapeDtypeStruct(terms.shape, jnp.float32),
            jax.ShapeDtypeStruct(right.shape, jnp.float32),
        ),
        in_specs=[pl.BlockSpec(memory_space=pltpu.VMEM)] * 3,
        out_specs=(pl.BlockSpec(memory_space=pltpu.VMEM),) * 2,
        input_output_aliases={2: 1},
        compiler_params=pltpu.CompilerParams(vmem_limit_bytes=VMEM_LIMIT),
    )(terms, weight, right)


def high_and_rest(x):
    high = x.astype(jnp.bfloat16)
    return high, (x - high.astype(jnp.float32)).astype(jnp.bfloat16)


def outer_kernel(left_ref, right_ref, o_ref):
    seqs, _, width_out = right_ref.shape
    for s in range(seqs):
        left_high, left_rest = high_and_rest(left_ref[s])
        right_high, right_rest = high_and_rest(right_ref[s])
        o_ref[pl.ds(s, width_out, stride=seqs), :] = lax.dot_general(
            jnp.concatenate([right_high, right_high, right_rest], axis=0),
            jnp.concatenate([left_high, left_rest, left_high], axis=0),
            (((0,), (0,)), ((), ())),
            preferred_element_type=jnp.float32,
        )


def outer(left, right):
    seqs, _, width_in = left.shape
    width_out = right.shape[2]
    return pl.pallas_call(
        outer_kernel,
        out_shape=jax.ShapeDtypeStruct((seqs * width_out, width_in), jnp.float32),
        in_specs=[pl.BlockSpec(memory_space=pltpu.VMEM)] * 2,
        out_specs=pl.BlockSpec(memory_space=pltpu.VMEM),
        compiler_params=pltpu.CompilerParams(vmem_limit_bytes=VMEM_LIMIT),
    )(left, right)


def expand_kernel(chips, map_ref, core_ref, own_ref, other_ref, o_ref):
    core = core_ref[0]
    owners = o_ref.shape[0] // 16
    pieces = owners // chips
    for n in range(owners):
        k = (2 * (n % chips) + core) * pieces + n // chips
        for side in range(2):
            at = pl.ds(pl.multiple_of(map_ref[side, k] * 8, 8), 8)
            o_ref[16 * n + 8 * side:16 * n + 8 * side + 8, :] = own_ref[at, :] + other_ref[at, :]


def expand(tile_map, core, own, other, owners, chips):
    return pl.pallas_call(
        functools.partial(expand_kernel, chips),
        out_shape=jax.ShapeDtypeStruct((owners * 16, own.shape[1]), jnp.float32),
        in_specs=[
            pl.BlockSpec(memory_space=pltpu.SMEM),
            pl.BlockSpec(memory_space=pltpu.SMEM),
            pl.BlockSpec(memory_space=pltpu.VMEM),
            pl.BlockSpec(memory_space=pltpu.VMEM),
        ],
        out_specs=pl.BlockSpec(memory_space=pltpu.VMEM),
        compiler_params=pltpu.CompilerParams(vmem_limit_bytes=VMEM_LIMIT),
    )(tile_map.T, core, own, other)


def covariance_kernel(terms_ref, prior_ref, o_ref):
    blocks = jnp.sum(terms_ref[...], axis=0)
    left = jnp.concatenate([blocks[0:4], blocks[4:8]], axis=1)
    right = jnp.concatenate([blocks[8:12], blocks[12:16]], axis=1)
    left_high, left_rest = high_and_rest(left)
    right_high, right_rest = high_and_rest(right)
    product = lax.dot_general(
        jnp.concatenate([left_high, left_high, left_rest], axis=0),
        jnp.concatenate([right_high, right_rest, right_high], axis=0),
        (((0,), (0,)), ((), ())),
        preferred_element_type=jnp.float32,
    )
    o_ref[0] = prior_ref[0] + product


def covariance(terms, prior_cov):
    return pl.pallas_call(
        covariance_kernel,
        out_shape=jax.ShapeDtypeStruct(prior_cov.shape, jnp.float32),
        in_specs=[pl.BlockSpec(memory_space=pltpu.VMEM)] * 2,
        out_specs=pl.BlockSpec(memory_space=pltpu.VMEM),
        compiler_params=pltpu.CompilerParams(vmem_limit_bytes=VMEM_LIMIT),
    )(terms, prior_cov)


def body(activations, out_grads, proj_in, proj_out, seq_lengths, tile_map, prior_cov):
    seqs, tok, _ = activations.shape
    width_in = proj_in.shape[1]
    pieces = lax.axis_size("tile")
    rows = seqs * tok // pieces
    owners = lax.axis_size("y") * pieces
    left = jnp.dot(activations.reshape(seqs * tok, -1), proj_in, preferred_element_type=jnp.float32)
    arrived = lax.all_to_all(left.reshape(pieces, rows, width_in), "tile", 0, 0, tiled=True)
    right = project(out_grads, proj_out)
    core = lax.axis_index("core")
    token = lax.axis_index("tile") * rows + jnp.arange(rows, dtype=jnp.int32)
    position = (lax.axis_index("y") * 2 + core) * tok + token % tok
    length = jnp.sum(jnp.where(token[:, None] // tok == jnp.arange(seqs)[None, :], seq_lengths[None, :], 0), axis=1)
    weight = jnp.where(position < length, lax.rsqrt(length.astype(jnp.float32)), 0.0)
    weight = jnp.broadcast_to(weight[:, None], (rows, width_in))
    arrived, right, weight = lax.optimization_barrier((arrived, right, weight))
    copies, right = combine(arrived, weight, right)
    left = lax.all_to_all(copies, "tile", 0, 0, tiled=True).reshape(seqs, tok, width_in)
    right = right.reshape(seqs, tok, -1)
    grads = outer(left, right)
    other = lax.ppermute(grads, "core", [(0, 1), (1, 0)])
    terms = expand(tile_map, core.reshape(1).astype(jnp.int32), grads, other, owners, lax.axis_size("y"))
    terms = lax.all_to_all(terms.reshape(owners, 16, width_in), ("tile", "y"), 0, 0, tiled=True)
    return covariance(terms, prior_cov)


def solution(mesh):
    layers, seq, tile = (mesh.shape[name] for name in ("layer", "seq", "tile"))
    fine = Mesh(mesh.devices.reshape(layers, seq // 2, 2, tile), ("layer", "y", "core", "tile"))
    split = ("y", "core")
    return jax.shard_map(
        body,
        mesh=fine,
        in_specs=(
            P("layer", split, "tile"),
            P("layer", split, "tile"),
            P(("layer", "tile"), None),
            P(("layer", "tile"), None),
            P(),
            P(),
            P(("layer", "y", "core", "tile"), None, None),
        ),
        out_specs=P(("layer", "y", "core", "tile"), None, None),
        check_vma=False,
    )
```

```python
import functools

import jax
import jax.numpy as jnp
from jax import lax
from jax.experimental import pallas as pl
from jax.experimental.pallas import tpu as pltpu
from jax.sharding import Mesh
from jax.sharding import PartitionSpec as P

PROJECT_VMEM = 60 * 1024 * 1024
VMEM_LIMIT = 4 * 1024 * 1024
ANY = pl.BlockSpec(memory_space=pl.ANY)
VMEM = pl.BlockSpec(memory_space=pltpu.VMEM)
SMEM = pl.BlockSpec(memory_space=pltpu.SMEM)
PARAMS = pltpu.CompilerParams(vmem_limit_bytes=VMEM_LIMIT)


def high_and_rest(x):
    high = x.astype(jnp.bfloat16)
    return high, (x - high.astype(jnp.float32)).astype(jnp.bfloat16)


def project_kernel(
    act_ref, grad_ref, in_ref, out_ref, len_ref, o_ref, weight_ref, act, grad, side_in, side_out, lengths, sems, grad_sems
):
    seqs, tok, _ = act.shape
    width_in = side_in.shape[1]
    rows = weight_ref.shape[0]
    half = seqs // 2
    copy_in = pltpu.make_async_copy(in_ref, side_in, sems.at[0])
    copy_act = pltpu.make_async_copy(act_ref, act, sems.at[1])
    copy_out = pltpu.make_async_copy(out_ref, side_out, sems.at[2])
    copy_len = pltpu.make_async_copy(len_ref, lengths, sems.at[3])
    parts = [pl.ds(part * half, half) for part in range(2)]
    copies = [pltpu.make_async_copy(grad_ref.at[p], grad.at[p], grad_sems.at[n]) for n, p in enumerate(parts)]
    copy_in.start()
    copy_act.start()
    copy_out.start()
    copy_len.start()
    for copy in copies:
        copy.start()
    copy_in.wait()
    copy_act.wait()
    for s in range(seqs):
        o_ref[s * tok:(s + 1) * tok, :width_in] = jnp.dot(
            act[s], side_in[...], preferred_element_type=jnp.float32
        )
    copy_out.wait()
    copy_len.wait()
    first = lax.axis_index("tile") * rows
    length = lengths[first // tok]
    position = (lax.axis_index("y") * 2 + lax.axis_index("core")) * tok + first % tok
    position = position + lax.broadcasted_iota(jnp.int32, weight_ref.shape, 0)
    scale = lax.rsqrt(jnp.full(weight_ref.shape, length, jnp.int32).astype(jnp.float32))
    weight_ref[...] = jnp.where(position < length, scale, 0.0)
    for part in range(2):
        copies[part].wait()
        for s in range(part * half, (part + 1) * half):
            o_ref[s * tok:(s + 1) * tok, width_in:] = jnp.dot(
                grad[s], side_out[...], preferred_element_type=jnp.float32
            )


def project(activations, out_grads, proj_in, proj_out, seq_lengths, rows):
    seqs, tok, dim = activations.shape
    hidden = out_grads.shape[2]
    width_in, width_out = proj_in.shape[1], proj_out.shape[1]
    width = width_in + width_out
    return pl.pallas_call(
        project_kernel,
        out_shape=(
            jax.ShapeDtypeStruct((seqs * tok, width), jnp.float32),
            jax.ShapeDtypeStruct((rows, width_in), jnp.float32),
        ),
        in_specs=[ANY] * 5,
        out_specs=(VMEM, VMEM),
        scratch_shapes=[
            pltpu.VMEM(activations.shape, activations.dtype),
            pltpu.VMEM(out_grads.shape, out_grads.dtype),
            pltpu.VMEM(proj_in.shape, proj_in.dtype),
            pltpu.VMEM(proj_out.shape, proj_out.dtype),
            pltpu.SMEM(seq_lengths.shape, seq_lengths.dtype),
            pltpu.SemaphoreType.DMA((4,)),
            pltpu.SemaphoreType.DMA((2,)),
        ],
        compiler_params=pltpu.CompilerParams(vmem_limit_bytes=PROJECT_VMEM),
        cost_estimate=pl.CostEstimate(
            flops=2 * seqs * tok * (dim * width_in + hidden * width_out),
            bytes_accessed=2 * seqs * tok * (dim + hidden) + 4 * seqs * tok * width,
            transcendentals=0,
        ),
    )(activations, out_grads, proj_in, proj_out, seq_lengths)


def combine_kernel(terms_ref, weight_ref, o_ref):
    width_in = weight_ref.shape[1]
    o_ref[:, :width_in] = jnp.sum(terms_ref[:, :, :width_in], axis=0) * weight_ref[...]
    o_ref[:, width_in:] = jnp.sum(terms_ref[:, :, width_in:], axis=0)


def combine(terms, weight):
    return pl.pallas_call(
        combine_kernel,
        out_shape=jax.ShapeDtypeStruct(terms.shape[1:], jnp.float32),
        in_specs=[VMEM] * 2,
        out_specs=VMEM,
        compiler_params=PARAMS,
    )(terms, weight)


def expand_kernel(chips, map_ref, own_ref, other_ref, o_ref, product_ref, blocks_ref):
    width_in = o_ref.shape[1]
    lefts, rights = [], []
    for ref in (own_ref, other_ref):
        left_high, left_rest = high_and_rest(ref[:, :width_in])
        right_high, right_rest = high_and_rest(ref[:, width_in:])
        lefts += [left_high, left_rest, left_high]
        rights += [right_high, right_high, right_rest]
    product_ref[...] = lax.dot_general(
        jnp.concatenate(rights, axis=0),
        jnp.concatenate(lefts, axis=0),
        (((0,), (0,)), ((), ())),
        preferred_element_type=jnp.float32,
    )
    count = product_ref.shape[0] // 2
    for r in range(2):
        rows = product_ref[pl.ds(r, count, stride=2), :]
        for again in range(4):
            blocks_ref[pl.ds(2 * again + r, count, stride=8), :] = rows
    core = lax.axis_index("core")
    owners = o_ref.shape[0] // 4
    pieces = owners // chips
    row = lax.broadcasted_iota(jnp.int32, (8, width_in), 0)
    for n in range(0, owners, 2):
        sides = []
        for owner in (n, n + 1):
            k = (2 * (owner % chips) + core) * pieces + owner // chips
            for side in range(2):
                sides.append(blocks_ref[pl.ds(pl.multiple_of(map_ref[side, k] * 8, 8), 8), :])
        low = jnp.where(row < 2, sides[0], sides[1])
        high = jnp.where(row < 6, sides[2], sides[3])
        o_ref[4 * n:4 * n + 8, :] = jnp.where(row < 4, low, high)


def expand(tile_map, own, other, width_in, owners, chips):
    width_out = own.shape[1] - width_in
    return pl.pallas_call(
        functools.partial(expand_kernel, chips),
        out_shape=jax.ShapeDtypeStruct((owners * 4, width_in), jnp.float32),
        in_specs=[SMEM, VMEM, VMEM],
        out_specs=VMEM,
        scratch_shapes=[
            pltpu.VMEM((width_out, width_in), jnp.float32),
            pltpu.VMEM((4 * width_out, width_in), jnp.float32),
        ],
        compiler_params=PARAMS,
    )(tile_map.T, own, other)


def covariance_kernel(terms_ref, prior_ref, o_ref):
    blocks = jnp.sum(terms_ref[...], axis=1)
    blocks = blocks[:, 0:4] + blocks[:, 4:8]
    left = jnp.concatenate([blocks[:, 0], blocks[:, 1]], axis=1)
    right = jnp.concatenate([blocks[:, 2], blocks[:, 3]], axis=1)
    left_high, left_rest = high_and_rest(left)
    right_high, right_rest = high_and_rest(right)
    product = lax.dot_general(
        jnp.concatenate([left_high, left_high, left_rest], axis=0),
        jnp.concatenate([right_high, right_rest, right_high], axis=0),
        (((0,), (0,)), ((), ())),
        preferred_element_type=jnp.float32,
    )
    o_ref[0] = prior_ref[0] + product


def covariance(terms, prior_cov):
    return pl.pallas_call(
        covariance_kernel,
        out_shape=jax.ShapeDtypeStruct(prior_cov.shape, jnp.float32),
        in_specs=[VMEM] * 2,
        out_specs=VMEM,
        compiler_params=PARAMS,
    )(terms, prior_cov)


def body(activations, out_grads, proj_in, proj_out, seq_lengths, tile_map, prior_cov):
    seqs, tok, _ = activations.shape
    width_in = proj_in.shape[1]
    pieces, chips = lax.axis_size("tile"), lax.axis_size("y")
    rows = seqs * tok // pieces
    owners = chips * pieces
    partial, weight = project(activations, out_grads, proj_in, proj_out, seq_lengths, rows)
    arrived = lax.all_to_all(partial.reshape(pieces, rows, -1), "tile", 0, 0, tiled=True)
    own = combine(arrived, weight)
    other = lax.ppermute(own, "core", [(0, 1), (1, 0)])
    terms = expand(tile_map, own, other, width_in, owners, chips)
    terms = lax.all_to_all(terms.reshape(owners, 4, width_in), ("tile", "y"), 0, 0, tiled=True)
    return covariance(terms.reshape(seqs, owners // (2 * seqs), 8, width_in), prior_cov)


def solution(mesh):
    layers, seq, tile = (mesh.shape[name] for name in ("layer", "seq", "tile"))
    fine = Mesh(mesh.devices.reshape(layers, seq // 2, 2, tile), ("layer", "y", "core", "tile"))
    tokens = P("layer", ("y", "core"), "tile")
    features = P(("layer", "tile"), None)
    tiles = P(("layer", "y", "core", "tile"), None, None)
    return jax.shard_map(
        body,
        mesh=fine,
        in_specs=(tokens, tokens, features, features, P(), P(), tiles),
        out_specs=tiles,
        check_vma=False,
    )
```

```python
import functools

import jax
import jax.numpy as jnp
from jax import lax
from jax.experimental import pallas as pl
from jax.experimental.pallas import tpu as pltpu
from jax.sharding import Mesh
from jax.sharding import PartitionSpec as P

PROJECT_VMEM = 60 * 1024 * 1024
VMEM_LIMIT = 4 * 1024 * 1024
ANY = pl.BlockSpec(memory_space=pl.ANY)
VMEM = pl.BlockSpec(memory_space=pltpu.VMEM)
SMEM = pl.BlockSpec(memory_space=pltpu.SMEM)
PARAMS = pltpu.CompilerParams(vmem_limit_bytes=VMEM_LIMIT)


def high_and_rest(x):
    high = x.astype(jnp.bfloat16)
    return high, (x - high.astype(jnp.float32)).astype(jnp.bfloat16)


def project_kernel(
    act_ref, grad_ref, in_ref, out_ref, len_ref, keep_ref, up_ref, down_ref,
    act, grad, side_in, side_out, lengths, held, sems, grad_sems, held_sems
):
    seqs, tok, _ = act.shape
    width_in = side_in.shape[1]
    rows = held.shape[1]
    half = seqs // 2
    pieces = held.shape[0]

    def store(s, columns, value):
        for part in range(tok // rows):
            ahead = lax.rem(s * (tok // rows) + part - lax.axis_index("tile") + pieces, pieces)
            slot = jnp.int32(0)
            for place, distance in enumerate((0, 1, 7, 4, 2, 5, 6, 3)):
                slot = jnp.where(ahead == distance, place, slot)
            held[slot, :, columns] = value[part * rows:(part + 1) * rows]

    copy_in = pltpu.make_async_copy(in_ref, side_in, sems.at[0])
    copy_act = pltpu.make_async_copy(act_ref, act, sems.at[1])
    copy_out = pltpu.make_async_copy(out_ref, side_out, sems.at[2])
    copy_len = pltpu.make_async_copy(len_ref, lengths, sems.at[3])
    parts = [pl.ds(part * half, half) for part in range(2)]
    copies = [pltpu.make_async_copy(grad_ref.at[p], grad.at[p], grad_sems.at[n]) for n, p in enumerate(parts)]
    copy_len.start()
    copy_in.start()
    copy_act.start()
    copy_out.start()
    for copy in copies:
        copy.start()
    position = lax.broadcasted_iota(jnp.int32, (tok, width_in), 0)
    position = position + (lax.axis_index("y") * 2 + lax.axis_index("core")) * tok
    copy_in.wait()
    copy_len.wait()
    copy_act.wait()
    for s in range(seqs):
        left = jnp.dot(act[s], side_in[...], preferred_element_type=jnp.float32)
        scale = lax.rsqrt(jnp.full(position.shape, lengths[s], jnp.int32).astype(jnp.float32))
        store(s, slice(0, width_in), left * jnp.where(position < lengths[s], scale, 0.0))
    copy_out.wait()
    for part in range(2):
        copies[part].wait()
        for s in range(part * half, (part + 1) * half):
            right = jnp.dot(grad[s], side_out[...], preferred_element_type=jnp.float32)
            store(s, slice(width_in, None), right)
    leave = [
        pltpu.make_async_copy(held.at[pl.ds(4, 2)], up_ref, held_sems.at[0]),
        pltpu.make_async_copy(held.at[pl.ds(6, 2)], down_ref, held_sems.at[1]),
        pltpu.make_async_copy(held.at[pl.ds(0, 4)], keep_ref, held_sems.at[2]),
    ]
    for copy in leave:
        copy.start()
    for copy in leave:
        copy.wait()


def project(activations, out_grads, proj_in, proj_out, seq_lengths, rows):
    seqs, tok, dim = activations.shape
    hidden = out_grads.shape[2]
    width_in, width_out = proj_in.shape[1], proj_out.shape[1]
    width = width_in + width_out
    return pl.pallas_call(
        project_kernel,
        out_shape=(
            jax.ShapeDtypeStruct((4, rows, width), jnp.float32),
            jax.ShapeDtypeStruct((2, rows, width), jnp.float32),
            jax.ShapeDtypeStruct((2, rows, width), jnp.float32),
        ),
        in_specs=[ANY] * 5,
        out_specs=(ANY,) * 3,
        scratch_shapes=[
            pltpu.VMEM(activations.shape, activations.dtype),
            pltpu.VMEM(out_grads.shape, out_grads.dtype),
            pltpu.VMEM(proj_in.shape, proj_in.dtype),
            pltpu.VMEM(proj_out.shape, proj_out.dtype),
            pltpu.SMEM(seq_lengths.shape, seq_lengths.dtype),
            pltpu.VMEM((8, rows, width), jnp.float32),
            pltpu.SemaphoreType.DMA((4,)),
            pltpu.SemaphoreType.DMA((2,)),
            pltpu.SemaphoreType.DMA((3,)),
        ],
        compiler_params=pltpu.CompilerParams(vmem_limit_bytes=PROJECT_VMEM),
        cost_estimate=pl.CostEstimate(
            flops=2 * seqs * tok * (dim * width_in + hidden * width_out),
            bytes_accessed=2 * seqs * tok * (dim + hidden) + 4 * seqs * tok * width,
            transcendentals=0,
        ),
    )(activations, out_grads, proj_in, proj_out, seq_lengths)


def hold_kernel(keep_ref, held_ref):
    pass


def hold(keep):
    return pl.pallas_call(
        hold_kernel,
        out_shape=jax.ShapeDtypeStruct(keep.shape, keep.dtype),
        in_specs=[VMEM],
        out_specs=VMEM,
        input_output_aliases={0: 0},
        compiler_params=PARAMS,
    )(keep)


def far_kernel(keep_ref, below_ref, above_ref, far_ref):
    far_ref[...] = keep_ref[3] + below_ref[1] + above_ref[1]


def near_kernel(keep_ref, below_ref, above_ref, far_ref, plus_ref, minus_ref):
    plus_ref[...] = keep_ref[1] + below_ref[0]
    minus_ref[...] = keep_ref[2] + above_ref[0]


def gather_far(keep, below, above):
    return pl.pallas_call(
        far_kernel,
        out_shape=jax.ShapeDtypeStruct(keep.shape[1:], jnp.float32),
        in_specs=[VMEM] * 3,
        out_specs=VMEM,
        compiler_params=PARAMS,
    )(keep, below, above)


def gather_near(keep, below, above, far):
    return pl.pallas_call(
        near_kernel,
        out_shape=(jax.ShapeDtypeStruct(keep.shape[1:], jnp.float32),) * 2,
        in_specs=[VMEM] * 4,
        out_specs=(VMEM,) * 2,
        compiler_params=PARAMS,
    )(keep, below, above, far)


def first_kernel(keep_ref, far_ref, o_ref):
    o_ref[...] = keep_ref[0] + far_ref[...]


def last_kernel(first_ref, plus_ref, minus_ref, o_ref):
    o_ref[...] = first_ref[...] + plus_ref[...] + minus_ref[...]


def combine(keep, far, plus, minus):
    piece = jax.ShapeDtypeStruct(plus.shape, jnp.float32)
    first = pl.pallas_call(
        first_kernel, out_shape=piece, in_specs=[VMEM] * 2, out_specs=VMEM, compiler_params=PARAMS
    )(keep, far)
    return pl.pallas_call(
        last_kernel, out_shape=piece, in_specs=[VMEM] * 3, out_specs=VMEM, compiler_params=PARAMS
    )(first, plus, minus)


def expand_kernel(chips, map_ref, own_ref, other_ref, o_ref, product_ref, blocks_ref):
    width_in = o_ref.shape[1]
    lefts, rights = [], []
    for ref in (own_ref, other_ref):
        left_high, left_rest = high_and_rest(ref[:, :width_in])
        right_high, right_rest = high_and_rest(ref[:, width_in:])
        lefts += [left_high, left_rest, left_high]
        rights += [right_high, right_high, right_rest]
    product_ref[...] = lax.dot_general(
        jnp.concatenate(rights, axis=0),
        jnp.concatenate(lefts, axis=0),
        (((0,), (0,)), ((), ())),
        preferred_element_type=jnp.float32,
    )
    count = product_ref.shape[0] // 2
    for r in range(2):
        rows = product_ref[pl.ds(r, count, stride=2), :]
        for again in range(4):
            blocks_ref[pl.ds(2 * again + r, count, stride=8), :] = rows
    core = lax.axis_index("core")
    owners = o_ref.shape[0] // 4
    pieces = owners // chips
    row = lax.broadcasted_iota(jnp.int32, (8, width_in), 0)
    for n in range(0, owners, 2):
        sides = []
        for owner in (n, n + 1):
            k = (2 * (owner % chips) + core) * pieces + owner // chips
            for side in range(2):
                sides.append(blocks_ref[pl.ds(pl.multiple_of(map_ref[side, k] * 8, 8), 8), :])
        low = jnp.where(row < 2, sides[0], sides[1])
        high = jnp.where(row < 6, sides[2], sides[3])
        o_ref[4 * n:4 * n + 8, :] = jnp.where(row < 4, low, high)


def expand(tile_map, own, other, width_in, owners, chips):
    width_out = own.shape[1] - width_in
    return pl.pallas_call(
        functools.partial(expand_kernel, chips),
        out_shape=jax.ShapeDtypeStruct((owners * 4, width_in), jnp.float32),
        in_specs=[SMEM, VMEM, VMEM],
        out_specs=VMEM,
        scratch_shapes=[
            pltpu.VMEM((width_out, width_in), jnp.float32),
            pltpu.VMEM((4 * width_out, width_in), jnp.float32),
        ],
        compiler_params=PARAMS,
    )(tile_map.T, own, other)


def covariance_kernel(terms_ref, prior_ref, o_ref):
    blocks = jnp.sum(terms_ref[...], axis=1)
    blocks = blocks[:, 0:4] + blocks[:, 4:8]
    left = jnp.concatenate([blocks[:, 0], blocks[:, 1]], axis=1)
    right = jnp.concatenate([blocks[:, 2], blocks[:, 3]], axis=1)
    left_high, left_rest = high_and_rest(left)
    right_high, right_rest = high_and_rest(right)
    product = lax.dot_general(
        jnp.concatenate([left_high, left_high, left_rest], axis=0),
        jnp.concatenate([right_high, right_rest, right_high], axis=0),
        (((0,), (0,)), ((), ())),
        preferred_element_type=jnp.float32,
    )
    o_ref[0] = prior_ref[0] + product


def covariance(terms, prior_cov):
    return pl.pallas_call(
        covariance_kernel,
        out_shape=jax.ShapeDtypeStruct(prior_cov.shape, jnp.float32),
        in_specs=[VMEM] * 2,
        out_specs=VMEM,
        compiler_params=PARAMS,
    )(terms, prior_cov)


def body(activations, out_grads, proj_in, proj_out, seq_lengths, tile_map, prior_cov):
    seqs, tok, _ = activations.shape
    width_in = proj_in.shape[1]
    pieces, chips = lax.axis_size("tile"), lax.axis_size("y")
    rows = seqs * tok // pieces
    owners = chips * pieces
    keep, up, down = project(activations, out_grads, proj_in, proj_out, seq_lengths, rows)

    def shift(x, by):
        return lax.ppermute(x, "tile", [(i, (i + by) % pieces) for i in range(pieces)])

    below, above = shift(up, 1), shift(down, -1)
    keep = hold(keep)
    far = gather_far(keep, below, above)
    plus, minus = gather_near(keep, below, above, far)
    far, plus, minus = shift(far, pieces // 2), shift(plus, 1), shift(minus, -1)
    own = combine(keep, far, plus, minus)
    other = lax.ppermute(own, "core", [(0, 1), (1, 0)])
    terms = expand(tile_map, own, other, width_in, owners, chips)
    terms = lax.all_to_all(terms.reshape(owners, 4, width_in), ("tile", "y"), 0, 0, tiled=True)
    return covariance(terms.reshape(seqs, owners // (2 * seqs), 8, width_in), prior_cov)


def solution(mesh):
    layers, seq, tile = (mesh.shape[name] for name in ("layer", "seq", "tile"))
    fine = Mesh(mesh.devices.reshape(layers, seq // 2, 2, tile), ("layer", "y", "core", "tile"))
    tokens = P("layer", ("y", "core"), "tile")
    features = P(("layer", "tile"), None)
    tiles = P(("layer", "y", "core", "tile"), None, None)
    return jax.shard_map(
        body,
        mesh=fine,
        in_specs=(tokens, tokens, features, features, P(), P(), tiles),
        out_specs=tiles,
        check_vma=False,
    )
```

```python
import functools

import jax
import jax.numpy as jnp
from jax import lax
from jax.experimental import pallas as pl
from jax.experimental.pallas import tpu as pltpu
from jax.sharding import Mesh
from jax.sharding import PartitionSpec as P

PROJECT_VMEM = 60 * 1024 * 1024
VMEM_LIMIT = 4 * 1024 * 1024
ANY = pl.BlockSpec(memory_space=pl.ANY)
VMEM = pl.BlockSpec(memory_space=pltpu.VMEM)
SMEM = pl.BlockSpec(memory_space=pltpu.SMEM)
PARAMS = pltpu.CompilerParams(vmem_limit_bytes=VMEM_LIMIT)


def high_and_rest(x):
    high = x.astype(jnp.bfloat16)
    return high, (x - high.astype(jnp.float32)).astype(jnp.bfloat16)


def project_kernel(
    act_ref, grad_ref, in_ref, out_ref, len_ref, keep_ref, up_ref, down_ref,
    act, grad, side_in, side_out, lengths, held, sems, grad_sems, held_sems
):
    seqs, tok, _ = act.shape
    width_in = side_in.shape[1]
    rows = held.shape[1]
    half = seqs // 2
    pieces = held.shape[0]

    def store(s, columns, value):
        for part in range(tok // rows):
            ahead = lax.rem(s * (tok // rows) + part - lax.axis_index("tile") + pieces, pieces)
            slot = jnp.int32(0)
            for place, distance in enumerate((0, 1, 7, 4, 2, 5, 6, 3)):
                slot = jnp.where(ahead == distance, place, slot)
            held[slot, :, columns] = value[part * rows:(part + 1) * rows]

    copy_in = pltpu.make_async_copy(in_ref, side_in, sems.at[0])
    copy_act = pltpu.make_async_copy(act_ref, act, sems.at[1])
    copy_out = pltpu.make_async_copy(out_ref, side_out, sems.at[2])
    copy_len = pltpu.make_async_copy(len_ref, lengths, sems.at[3])
    spans = [(0, half)] + [(s, s + 1) for s in range(half, seqs)]
    parts = [pl.ds(start, stop - start) for start, stop in spans]
    copies = [pltpu.make_async_copy(grad_ref.at[p], grad.at[p], grad_sems.at[n]) for n, p in enumerate(parts)]
    copy_len.start()
    copy_in.start()
    copy_act.start()
    copy_out.start()
    for copy in copies:
        copy.start()
    position = lax.broadcasted_iota(jnp.int32, (tok, width_in), 0)
    position = position + (lax.axis_index("y") * 2 + lax.axis_index("core")) * tok
    copy_in.wait()
    copy_len.wait()
    copy_act.wait()
    for s in range(seqs):
        left = jnp.dot(act[s], side_in[...], preferred_element_type=jnp.float32)
        scale = lax.rsqrt(jnp.full(position.shape, lengths[s], jnp.int32).astype(jnp.float32))
        store(s, slice(0, width_in), left * jnp.where(position < lengths[s], scale, 0.0))
    copy_out.wait()
    for copy, (start, stop) in zip(copies, spans):
        copy.wait()
        for s in range(start, stop):
            right = jnp.dot(grad[s], side_out[...], preferred_element_type=jnp.float32)
            store(s, slice(width_in, None), right)
    leave = [
        pltpu.make_async_copy(held.at[pl.ds(4, 2)], up_ref, held_sems.at[0]),
        pltpu.make_async_copy(held.at[pl.ds(6, 2)], down_ref, held_sems.at[1]),
        pltpu.make_async_copy(held.at[pl.ds(0, 4)], keep_ref, held_sems.at[2]),
    ]
    for copy in leave:
        copy.start()
    for copy in leave:
        copy.wait()


def project(activations, out_grads, proj_in, proj_out, seq_lengths, rows):
    seqs, tok, dim = activations.shape
    hidden = out_grads.shape[2]
    width_in, width_out = proj_in.shape[1], proj_out.shape[1]
    width = width_in + width_out
    return pl.pallas_call(
        project_kernel,
        out_shape=(
            jax.ShapeDtypeStruct((4, rows, width), jnp.float32),
            jax.ShapeDtypeStruct((2, rows, width), jnp.float32),
            jax.ShapeDtypeStruct((2, rows, width), jnp.float32),
        ),
        in_specs=[ANY] * 5,
        out_specs=(ANY,) * 3,
        scratch_shapes=[
            pltpu.VMEM(activations.shape, activations.dtype),
            pltpu.VMEM(out_grads.shape, out_grads.dtype),
            pltpu.VMEM(proj_in.shape, proj_in.dtype),
            pltpu.VMEM(proj_out.shape, proj_out.dtype),
            pltpu.SMEM(seq_lengths.shape, seq_lengths.dtype),
            pltpu.VMEM((8, rows, width), jnp.float32),
            pltpu.SemaphoreType.DMA((4,)),
            pltpu.SemaphoreType.DMA((1 + seqs - seqs // 2,)),
            pltpu.SemaphoreType.DMA((3,)),
        ],
        compiler_params=pltpu.CompilerParams(vmem_limit_bytes=PROJECT_VMEM),
        cost_estimate=pl.CostEstimate(
            flops=2 * seqs * tok * (dim * width_in + hidden * width_out),
            bytes_accessed=2 * seqs * tok * (dim + hidden) + 4 * seqs * tok * width,
            transcendentals=0,
        ),
    )(activations, out_grads, proj_in, proj_out, seq_lengths)


def hold_kernel(keep_ref, held_ref):
    pass


def hold(keep):
    return pl.pallas_call(
        hold_kernel,
        out_shape=jax.ShapeDtypeStruct(keep.shape, keep.dtype),
        in_specs=[VMEM],
        out_specs=VMEM,
        input_output_aliases={0: 0},
        compiler_params=PARAMS,
    )(keep)


def far_kernel(keep_ref, below_ref, above_ref, far_ref):
    far_ref[...] = keep_ref[3] + below_ref[1] + above_ref[1]


def near_kernel(keep_ref, below_ref, above_ref, far_ref, plus_ref, minus_ref):
    plus_ref[...] = keep_ref[1] + below_ref[0]
    minus_ref[...] = keep_ref[2] + above_ref[0]


def gather_far(keep, below, above):
    return pl.pallas_call(
        far_kernel,
        out_shape=jax.ShapeDtypeStruct(keep.shape[1:], jnp.float32),
        in_specs=[VMEM] * 3,
        out_specs=VMEM,
        compiler_params=PARAMS,
    )(keep, below, above)


def gather_near(keep, below, above, far):
    return pl.pallas_call(
        near_kernel,
        out_shape=(jax.ShapeDtypeStruct(keep.shape[1:], jnp.float32),) * 2,
        in_specs=[VMEM] * 4,
        out_specs=(VMEM,) * 2,
        compiler_params=PARAMS,
    )(keep, below, above, far)


def first_kernel(keep_ref, far_ref, o_ref):
    o_ref[...] = keep_ref[0] + far_ref[...]


def last_kernel(first_ref, plus_ref, minus_ref, o_ref):
    o_ref[...] = first_ref[...] + plus_ref[...] + minus_ref[...]


def combine(keep, far, plus, minus):
    piece = jax.ShapeDtypeStruct(plus.shape, jnp.float32)
    first = pl.pallas_call(
        first_kernel, out_shape=piece, in_specs=[VMEM] * 2, out_specs=VMEM, compiler_params=PARAMS
    )(keep, far)
    return pl.pallas_call(
        last_kernel, out_shape=piece, in_specs=[VMEM] * 3, out_specs=VMEM, compiler_params=PARAMS
    )(first, plus, minus)


def expand_kernel(chips, map_ref, own_ref, other_ref, o_ref, product_ref, blocks_ref):
    width_in = o_ref.shape[1]
    lefts, rights = [], []
    for ref in (own_ref, other_ref):
        left_high, left_rest = high_and_rest(ref[:, :width_in])
        right_high, right_rest = high_and_rest(ref[:, width_in:])
        lefts += [left_high, left_rest, left_high]
        rights += [right_high, right_high, right_rest]
    product_ref[...] = lax.dot_general(
        jnp.concatenate(rights, axis=0),
        jnp.concatenate(lefts, axis=0),
        (((0,), (0,)), ((), ())),
        preferred_element_type=jnp.float32,
    )
    count = product_ref.shape[0] // 2
    for r in range(2):
        rows = product_ref[pl.ds(r, count, stride=2), :]
        for again in range(4):
            blocks_ref[pl.ds(2 * again + r, count, stride=8), :] = rows
    core = lax.axis_index("core")
    owners = o_ref.shape[0] // 4
    pieces = owners // chips
    row = lax.broadcasted_iota(jnp.int32, (8, width_in), 0)
    for n in range(0, owners, 2):
        sides = []
        for owner in (n, n + 1):
            k = (2 * (owner % chips) + core) * pieces + owner // chips
            for side in range(2):
                sides.append(blocks_ref[pl.ds(pl.multiple_of(map_ref[side, k] * 8, 8), 8), :])
        low = jnp.where(row < 2, sides[0], sides[1])
        high = jnp.where(row < 6, sides[2], sides[3])
        o_ref[4 * n:4 * n + 8, :] = jnp.where(row < 4, low, high)


def expand(tile_map, own, other, width_in, owners, chips):
    width_out = own.shape[1] - width_in
    return pl.pallas_call(
        functools.partial(expand_kernel, chips),
        out_shape=jax.ShapeDtypeStruct((owners * 4, width_in), jnp.float32),
        in_specs=[SMEM, VMEM, VMEM],
        out_specs=VMEM,
        scratch_shapes=[
            pltpu.VMEM((width_out, width_in), jnp.float32),
            pltpu.VMEM((4 * width_out, width_in), jnp.float32),
        ],
        compiler_params=PARAMS,
    )(tile_map.T, own, other)


def covariance_kernel(terms_ref, prior_ref, o_ref):
    blocks = jnp.sum(terms_ref[...], axis=1)
    blocks = blocks[:, 0:4] + blocks[:, 4:8]
    left = jnp.concatenate([blocks[:, 0], blocks[:, 1]], axis=1)
    right = jnp.concatenate([blocks[:, 2], blocks[:, 3]], axis=1)
    left_high, left_rest = high_and_rest(left)
    right_high, right_rest = high_and_rest(right)
    product = lax.dot_general(
        jnp.concatenate([left_high, left_high, left_rest], axis=0),
        jnp.concatenate([right_high, right_rest, right_high], axis=0),
        (((0,), (0,)), ((), ())),
        preferred_element_type=jnp.float32,
    )
    o_ref[0] = prior_ref[0] + product


def covariance(terms, prior_cov):
    return pl.pallas_call(
        covariance_kernel,
        out_shape=jax.ShapeDtypeStruct(prior_cov.shape, jnp.float32),
        in_specs=[VMEM] * 2,
        out_specs=VMEM,
        compiler_params=PARAMS,
    )(terms, prior_cov)


def body(activations, out_grads, proj_in, proj_out, seq_lengths, tile_map, prior_cov):
    seqs, tok, _ = activations.shape
    width_in = proj_in.shape[1]
    pieces, chips = lax.axis_size("tile"), lax.axis_size("y")
    rows = seqs * tok // pieces
    owners = chips * pieces
    keep, up, down = project(activations, out_grads, proj_in, proj_out, seq_lengths, rows)

    def shift(x, by):
        return lax.ppermute(x, "tile", [(i, (i + by) % pieces) for i in range(pieces)])

    below, above = shift(up, 1), shift(down, -1)
    keep = hold(keep)
    far = gather_far(keep, below, above)
    plus, minus = gather_near(keep, below, above, far)
    far, plus, minus = shift(far, pieces // 2), shift(plus, 1), shift(minus, -1)
    own = combine(keep, far, plus, minus)
    other = lax.ppermute(own, "core", [(0, 1), (1, 0)])
    terms = expand(tile_map, own, other, width_in, owners, chips)
    terms = lax.all_to_all(terms.reshape(owners, 4, width_in), ("tile", "y"), 0, 0, tiled=True)
    return covariance(terms.reshape(seqs, owners // (2 * seqs), 8, width_in), prior_cov)


def solution(mesh):
    layers, seq, tile = (mesh.shape[name] for name in ("layer", "seq", "tile"))
    fine = Mesh(mesh.devices.reshape(layers, seq // 2, 2, tile), ("layer", "y", "core", "tile"))
    tokens = P("layer", ("y", "core"), "tile")
    features = P(("layer", "tile"), None)
    tiles = P(("layer", "y", "core", "tile"), None, None)
    return jax.shard_map(
        body,
        mesh=fine,
        in_specs=(tokens, tokens, features, features, P(), P(), tiles),
        out_specs=tiles,
        check_vma=False,
    )
```
